256 devices in a mesh: lon: 128 (over y, z, x_hi, core), tm: 2 (over x_lo).
Axes of the slice: x: 4 (x_hi: 2, x_lo: 2; x = x_hi * 2 + x_lo), y: 4, z: 8, core: 2. Of those that a mesh axis runs over, the one named last changes fastest.
Arguments:
- video: bfloat16 [8, 8, 1024, 384], P('tm', None, 'lon'), may hold values from -6 to 6
- gain_one: float32 [384], replicated, may hold values from 0.1 to 1.9
- weight_one: bfloat16 [27, 384, 384], P(None, 'lon'), may hold values from -0.0625 to 0.0625
- bias_one: float32 [384], replicated, may hold values from -3 to 3
- gain_two: float32 [384], replicated, may hold values from 0.1 to 1.9
- weight_two: bfloat16 [27, 384, 384], P(None, 'lon'), may hold values from -0.0625 to 0.0625
- bias_two: float32 [384], replicated, may hold values from -2 to 2
- cache_one: bfloat16 [2, 8, 1024, 384], P(None, None, 'lon'), may hold values from -6 to 6
- cache_two: bfloat16 [2, 8, 1024, 384], P(None, None, 'lon'), may hold values from -6 to 6
Outputs:
- result: bfloat16 [8, 8, 1024, 384], P('tm', None, 'lon')
The draws below stay inside these ranges and needn't reach their ends.
All inputs are finite; a program needn't handle non-finite values.
Results may differ from the reference program's by a relative error of at most 0.0033.
Values may be sent and summed in bfloat16 or wider, within the bound.
No kernel may reach another device: no remote copies, remote signals or barrier semaphores. Data moves between devices by JAX's collectives and lax.ppermute only.
A program may use at most 128 MiB of HBM per device.

```python
import jax
import jax.numpy as jnp
from jax import lax

C = 384
LAT = 8
FRAMES = 8
LONS = 1024


def shard_levels(key, extent, shards, smallest, largest):
    level = 1.0
    for axis_at, parts in shards:
        heights = jax.random.uniform(jax.random.fold_in(jax.random.fold_in(key, 6), axis_at), (parts,), jnp.float32, smallest / len(shards), largest / len(shards))
        level = level * jnp.repeat(jnp.exp(heights), extent[axis_at] // parts).reshape((-1,) + (1,) * (len(extent) - 1 - axis_at))
    return level


def noise(stream_key, extent, scale, limit, cuts=(), held_as=jnp.bfloat16):
    entries = scale * jax.random.normal(stream_key, extent, jnp.float32)
    if cuts:
        entries = entries * shard_levels(stream_key, extent, cuts, -0.22, 0.18)
    return jnp.clip(entries, -limit, limit).astype(held_as)


def setup_inputs(seed: int = 0) -> dict:
    streams_of = jax.random.split(jax.random.key(seed), 10)
    return {
        "video": noise(streams_of[0], (FRAMES, LAT, LONS, C), 1.0, 6.0, ((0, 2), (2, 128))),
        "gain_one": jnp.clip(1.0 + 0.18 * jax.random.normal(streams_of[1], (C,), jnp.float32), 0.1, 1.9),
        "weight_one": noise(streams_of[2], (27, C, C), (27 * C) ** -0.5, 0.0625, ((1, 128),)),
        "bias_one": noise(streams_of[3], (C,), 0.5, 3.0, (), jnp.float32),
        "gain_two": jnp.clip(1.0 + 0.18 * jax.random.normal(streams_of[4], (C,), jnp.float32), 0.1, 1.9),
        "weight_two": noise(streams_of[5], (27, C, C), (27 * C) ** -0.5, 0.0625, ((1, 128),)),
        "bias_two": noise(streams_of[6], (C,), 0.3, 2.0, (), jnp.float32),
        "cache_one": noise(streams_of[7], (2, LAT, LONS, C), 1.0, 6.0, ((2, 128),)),
        "cache_two": noise(streams_of[8], (2, LAT, LONS, C), 1.0, 6.0, ((2, 128),)),
    }


def norm_silu(values, gain):
    square = lax.optimization_barrier(jnp.mean(values * values, axis=-1, keepdims=True))
    scaled = values * lax.rsqrt(square + 1e-06) * gain
    return jax.nn.silu(scaled).astype(jnp.bfloat16)

def convolve(padded, weights, offset):
    padded = jnp.pad(padded, ((0, 0), (1, 1), (0, 0), (0, 0)))
    frames_out = padded.shape[0] - 2
    lat_rows = padded.shape[1] - 2
    columns = padded.shape[2] - 2
    channels = padded.shape[3]
    total_sum = jnp.zeros((frames_out * lat_rows * columns, weights.shape[-1]), jnp.float32)
    for frame_tap in range(3):
        for row_tap in range(3):
            for column_tap in range(3):
                window = padded[frame_tap:frame_tap + frames_out, row_tap:row_tap + lat_rows, column_tap:column_tap + columns]
                kernel = weights[9 * frame_tap + 3 * row_tap + column_tap]
                total_sum = total_sum + jnp.dot(window.reshape(-1, channels), kernel, preferred_element_type=jnp.float32)
    return total_sum.reshape(frames_out, lat_rows, columns, -1) + offset

def wrap_columns(field):
    return jnp.concatenate([field[:, :, -1:], field, field[:, :, :1]], axis=2)

def reference(video, gain_one, weight_one, bias_one, gain_two, weight_two, bias_two, cache_one, cache_two):
    first_in = norm_silu(video.astype(jnp.float32), gain_one)
    hidden = convolve(wrap_columns(jnp.concatenate([cache_one, first_in], axis=0)), weight_one, bias_one)
    second_in = norm_silu(hidden, gain_two)
    branch = convolve(wrap_columns(jnp.concatenate([cache_two, second_in], axis=0)), weight_two, bias_two)
    return (video.astype(jnp.float32) + branch).astype(jnp.bfloat16)
```

```python
import jax
import jax.numpy as jnp
from jax import lax
from jax.experimental import pallas as pl
from jax.experimental.pallas import tpu as pltpu
from jax.sharding import Mesh
from jax.sharding import PartitionSpec as P

LON = ("y", "z", "xh", "core")
RING = ("xh", "core", "tm")
PLANE = ("y", "z")
F32 = jnp.float32
BF16 = jnp.bfloat16
MIB = 1 << 20


def lanes(shape):
    return lax.broadcasted_iota(jnp.int32, shape, len(shape) - 1)


def half_roll(x):
    return pltpu.roll(x, 64, x.ndim - 1)


def norm_silu(x, gain):
    square = jnp.mean(x * x, axis=-1, keepdims=True)
    scaled = x * lax.rsqrt(square + 1e-06) * gain
    return scaled / (1.0 + jnp.exp(-scaled))


def put(wide, at, value):
    for k in range(3):
        wide[k, at : at + value.shape[0]] = value[:, 128 * k : 128 * k + 128]


def every(wide, start, step):
    return jnp.concatenate([wide[k, pl.ds(start, 8, stride=step), :] for k in range(3)], axis=1)


def spread_matrix():
    row = lax.broadcasted_iota(jnp.int32, (384, 512), 0)
    k = lax.broadcasted_iota(jnp.int32, (384, 512), 1)
    q, r, yz = k >> 7, (k >> 5) & 3, k & 31
    return jnp.where((row == 12 * yz + 3 * q + r) & (r < 3), 1.0, 0.0)


def order_matrix():
    row = lax.broadcasted_iota(jnp.int32, (384, 384), 0)
    k = lax.broadcasted_iota(jnp.int32, (384, 384), 1)
    r, z, y, q = k >> 7, (k >> 4) & 7, (k >> 2) & 3, k & 3
    return jnp.where(row == 96 * y + 12 * z + 3 * q + r, 1.0, 0.0)


def pack(slot, taps, half):
    first = half == 0
    low_lanes = lanes((14, 128)) < 64
    for r, w in enumerate(taps):
        slot[pl.ds(r, 27, stride=3), :] = jnp.where(first, w[:, :128], w[:, 128:256])
        rest = w[:, 256:]
        turned = half_roll(rest)
        low = jnp.where(first, rest, turned)[:14]
        high = jnp.concatenate([jnp.where(first, turned, rest)[14:], jnp.zeros((1, 128), F32)], axis=0)
        slot[pl.ds(81 + r, 14, stride=3), :] = jnp.where(low_lanes, low, high)
    slot[123:] = jnp.zeros((5, 128), F32)


def send_kernel(ids, w1, w2, video, cache1, cache2, out1, out2, out_edge, slot, wide, edge):
    taps2 = [w2[r].astype(F32) for r in range(3)]
    for half in range(2):
        pack(slot, taps2, half)
        packed = slot[...].astype(BF16)
        for n in range(8):
            out2[2 * n + half] = packed
    order = order_matrix().astype(BF16)
    taps1 = [jnp.dot(w1[r], order, preferred_element_type=F32) for r in range(3)]
    pack(slot, taps1, ids[1])
    packed = slot[:124].astype(BF16)
    for n in range(8):
        out1[n] = packed

    upper = ids[0] == 1
    put(wide, 0, video[...].astype(F32).reshape(256, 384))
    put(wide, 256, cache1[ids[1]].astype(F32).reshape(64, 384))
    put(wide, 320, cache2[...].astype(F32).reshape(128, 384))

    def column(f, low, high):
        return jnp.where(upper, every(wide, 64 * f + high, 8), every(wide, 64 * f + low, 8))

    for c in range(2):
        for f in range(5):
            at = 40 * c + 8 * f
            edge[at : at + 8] = column(f, c, 6 + c)
    for f in range(2):
        edge[80 + 8 * f : 88 + 8 * f] = column(5 + f, 0, 7)
    out_edge[...] = edge[...].astype(BF16)


def turn_kernel(x, out, wide):
    wide[...] = x[...].astype(F32).reshape(2048, 128)

    def step(row, carry):
        out[row] = wide[pl.ds(row, 16, stride=128), :].astype(BF16)
        return carry

    lax.fori_loop(0, 128, step, 0, unroll=8)


def by_slice(x, gain):
    frame = lax.rem(lax.broadcasted_iota(jnp.int32, x.shape, 0) >> 3, 5)
    x = jnp.where(frame == 4, x, norm_silu(x, gain)).astype(BF16)
    return jnp.dot(x, spread_matrix().astype(BF16), preferred_element_type=F32).astype(BF16)


def ordered(x):
    return jnp.dot(x.astype(BF16), order_matrix().astype(BF16), preferred_element_type=F32).astype(BF16)


def own_kernel(ids, video, cache1, cache2, gain1, bias1, gain2, out, out_cache, out_vec, wide, rows):
    put(wide, 0, video[...].astype(F32).reshape(256, 384))
    put(wide, 256, cache1[ids[1]].astype(F32).reshape(64, 384))
    put(wide, 320, cache2[...].astype(F32).reshape(128, 384))
    for c in range(8):
        for f in range(5):
            at = 40 * c + 8 * f
            rows[at : at + 8] = every(wide, 64 * f + c, 8)
    slices = by_slice(rows[...], gain1[...].reshape(1, 384))
    for q in range(4):
        out[q] = slices[:, 128 * q : 128 * q + 128]
    for c in range(8):
        for f in range(2):
            at = 16 * c + 8 * f
            rows[at : at + 8] = every(wide, 320 + 64 * f + c, 8)
    out_cache[...] = ordered(rows[0:128]).reshape(8, 16, 384)
    vectors = jnp.concatenate(
        [bias1[...].reshape(1, 384), gain2[...].reshape(1, 384), gain1[...].reshape(1, 384), jnp.zeros((5, 384), F32)],
        axis=0,
    )
    placed = jnp.dot(vectors, order_matrix(), preferred_element_type=F32, precision=lax.Precision.HIGHEST)
    out_vec[...] = jnp.concatenate([placed[:2], vectors[2:]], axis=0)


def enter_kernel(ids, own, cache, vec, halo, out, out_cache):
    slices = by_slice(halo[0:80].astype(F32), vec[2:3])
    for q in range(4):
        for tm in range(2):
            out[2 * q + tm, 0:320] = own[q]
            out[2 * q + tm, 320:400] = slices[:, 128 * q : 128 * q + 128]
    beyond = ordered(halo[80:96])

    @pl.when(ids[0] == 0)
    def _():
        out_cache[0] = beyond
        out_cache[1:9] = cache[...]

    @pl.when(ids[0] == 1)
    def _():
        out_cache[0:8] = cache[...]
        out_cache[8] = beyond


def shifted_rows(x, p):
    if p == 1:
        return x
    axis = x.ndim - 2
    lat = lax.broadcasted_iota(jnp.int32, x.shape, axis)
    if p == 0:
        return jnp.where(lat == 0, 0.0, pltpu.roll(x, 1, axis))
    return jnp.where(lat == 7, 0.0, pltpu.roll(x, 7, axis))


def tap_of(t):
    return t // 9, (t // 3) % 3, t % 3


def first_kernel(ids, x, w0, w1, w2, w3, out_own, out_peer, field, even, odd, wide, kernel, part_a, part_b):
    for s in range(8):
        q, tm = s // 2, s % 2
        piece = x[s].astype(F32).reshape(10, 5, 8, 128)
        places = [(2 + 8 * q, 0, 8)]
        if q == 0:
            places.append((0, 8, 10))
        if q == 3:
            places.append((34, 8, 10))
        for at, begin, end in places:
            n = end - begin
            field[at : at + n, 2 + 4 * tm : 6 + 4 * tm] = piece[begin:end, 0:4]
            field[at : at + n, tm] = piece[begin:end, 4]

    def spread(c, carry):
        plane = field[c]
        for p in range(3):
            moved = shifted_rows(plane, p)
            even[p, c] = moved.reshape(80, 128).astype(BF16)
            odd[p, c] = moved[1:9].reshape(64, 128).astype(BF16)
        return carry

    lax.fori_loop(0, 36, spread, 0, unroll=4)

    for d, w in enumerate((w0, w1, w2, w3)):
        at = pl.multiple_of(1024 * ((ids[3] + 4 - d) & 3), 1024)
        for z in range(8):
            wide[pl.ds(at + 128 * z, 124), :] = w[z].astype(F32)
    for t in range(27):
        for r in range(3):
            kernel[t, 32 * r : 32 * r + 32, 0:128] = wide[pl.ds(3 * t + r, 32, stride=128), :].astype(BF16)
            kernel[t, 32 * r : 32 * r + 32, 128:256] = wide[
                pl.ds(81 + 3 * (t % 14) + r, 32, stride=128), :
            ].astype(BF16)
        kernel[t, 96:128] = jnp.zeros((32, 256), BF16)

    block = 34

    def multiply(i, carry):
        at = i * block

        def window(t):
            a, p, q = tap_of(t)
            if a == 1:
                rows = odd[p, pl.ds(at + q, block)]
            else:
                rows = even[p, pl.ds(at + q, block), 8 * a : 8 * a + 64]
            return rows.reshape(block * 64, 128)

        def total(taps):
            left = jnp.concatenate([window(t) for t in taps], axis=1)
            right = kernel[taps[0] : taps[-1] + 1].reshape(128 * len(taps), 256)
            return jnp.dot(left, right, preferred_element_type=F32)

        low = total(range(0, 14))
        high = total(range(14, 27))
        part_a[pl.ds(at, block)] = (low[:, :128] + high[:, :128]).reshape(block, 64, 128)
        part_b[pl.ds(at, block)] = (low[:, 128:] + half_roll(high[:, 128:])).reshape(block, 64, 128)
        return carry

    lax.fori_loop(0, 34 // block, multiply, 0)

    low_lanes = lanes((48, 128)) < 64
    for d in range(4):
        xh, tm = d // 2, d % 2
        for out, core in ((out_own, ids[0]), (out_peer, 1 - ids[0])):
            base = 16 * xh + 9 * core

            def rows_of(part, c):
                if tm == 1:
                    return part[c, 16:64]
                return jnp.concatenate([jnp.zeros((16, 128), F32), part[c, 0:32]], axis=0)

            for j in range(9):
                out[d, j] = rows_of(part_a, base + j).astype(BF16)
            for j in range(5):
                b = rows_of(part_b, base + j)
                if j < 4:
                    b = jnp.where(low_lanes, b, half_roll(rows_of(part_b, base + j + 5)))
                out[d, 9 + j] = b.astype(BF16)


def add_kernel(ids, x, y, *outs):
    for n, out in enumerate(outs):
        d = 2 * (ids[2] ^ (n >> 1)) + (ids[1] ^ (n & 1))

        def step(j, carry):
            out[j] = (x[d, j].astype(F32) + y[d, j].astype(F32)).astype(BF16)
            return carry

        lax.fori_loop(0, 14, step, 0, unroll=2)


def middle_kernel(ids, x0, x1, x2, x3, vec, cache, out):
    low_lanes = lanes((48, 128)) < 64
    starts = ids[1] == 0
    bias, gain = vec[0:1], vec[1:2]

    def summed(tm, j):
        mine = x0[j].astype(F32) + x2[j].astype(F32)
        other = x1[j].astype(F32) + x3[j].astype(F32)
        return jnp.where(ids[1] == tm, mine, other)

    for j in range(5):
        b0, b1 = summed(0, 9 + j), summed(1, 9 + j)
        places = [(j, jnp.where(low_lanes, b0, half_roll(b1)))]
        if j < 4:
            places.append((j + 5, jnp.where(low_lanes, half_roll(b0), b1)))
        for c, b in places:
            hidden = jnp.concatenate([summed(0, c), summed(1, c), b], axis=1) + bias
            normed = norm_silu(hidden, gain).astype(BF16)
            out[c, 16:48] = normed[16:48]
            out[c, 0:16] = jnp.where(starts, cache[c], normed[0:16])


def second_kernel(ids, x, w, bias, out_own, out_peer, even, odd, low, high):
    def spread(c, carry):
        plane = x[c].astype(F32).reshape(6, 8, 384)
        for p in range(3):
            moved = shifted_rows(plane, p)
            even[p, c] = moved.reshape(48, 384).astype(BF16)
            odd[p, c] = moved[1:5].reshape(32, 384).astype(BF16)
        return carry

    lax.fori_loop(0, 18, spread, 0, unroll=2)

    def window(t):
        a, p, q = tap_of(t)
        if a == 1:
            rows = odd[p, q : q + 16]
        else:
            rows = even[p, q : q + 16, 8 * a : 8 * a + 32]
        return rows.reshape(512, 384)

    def kernel(t):
        a = [w[:, 3 * t + r].reshape(128, 128) for r in range(3)]
        b = [w[:, 81 + 3 * (t % 14) + r].reshape(128, 128) for r in range(3)]
        return jnp.concatenate([jnp.concatenate(a, axis=0), jnp.concatenate(b, axis=0)], axis=1)

    for begin, end, total in ((0, 14, low), (14, 27, high)):
        for t in range(begin, end, 2):
            taps = range(t, min(t + 2, end))
            left = jnp.concatenate([window(s) for s in taps], axis=1)
            right = jnp.concatenate([kernel(s) for s in taps], axis=0)
            product = jnp.dot(left, right, preferred_element_type=F32)
            if t == begin:
                total[...] = product
            else:
                total[...] += product

    first = ids[0] == 0
    bias = bias[...].reshape(1, 384)
    rest = bias[:, 256:]
    bias_a = jnp.where(first, bias[:, :128], bias[:, 128:256])
    bias_b = jnp.where(first, rest, half_roll(rest))
    low[:, :128] = low[:, :128] + high[:, :128] + bias_a
    low[:, 128:] = low[:, 128:] + half_roll(high[:, 128:]) + bias_b
    own = pl.multiple_of(256 * ids[0], 256)
    peer = pl.multiple_of(256 - 256 * ids[0], 256)
    out_own[...] = low[pl.ds(own, 256)]
    out_peer[...] = low[pl.ds(peer, 256)]


def last_kernel(ids, own, peer, video, out, rows):
    first = ids[0] == 0
    low_lanes = lanes((256, 128)) < 64
    rows[0] = jnp.where(first, own[:, :128], peer[:, :128])
    rows[1] = jnp.where(first, peer[:, :128], own[:, :128])
    b0 = jnp.where(first, own[:, 128:], peer[:, 128:])
    b1 = jnp.where(first, peer[:, 128:], own[:, 128:])
    rows[2] = jnp.where(low_lanes, b0, half_roll(b1))
    for f in range(4):
        for i in range(8):
            branch = every(rows, 8 * f + i, 32)
            out[f, i] = (video[f, i].astype(F32) + branch).astype(BF16)


def run(kernel, outs, scratch, args, scalars=1, flops=0, limit=48):
    specs = [pl.BlockSpec(memory_space=pltpu.SMEM)] * scalars
    specs += [pl.BlockSpec(memory_space=pltpu.VMEM)] * (len(args) - scalars)
    moved = sum(a.size * a.dtype.itemsize for a in args[scalars:])
    return pl.pallas_call(
        kernel,
        out_shape=outs,
        in_specs=specs,
        out_specs=jax.tree.map(lambda _: pl.BlockSpec(memory_space=pltpu.VMEM), outs),
        scratch_shapes=scratch,
        compiler_params=pltpu.CompilerParams(vmem_limit_bytes=limit * MIB),
        cost_estimate=pl.CostEstimate(flops=flops, bytes_accessed=moved, transcendentals=0),
    )(*args)


def shape(*dims, dtype=BF16):
    return jax.ShapeDtypeStruct(dims, dtype)


def per_device(video, gain1, w1, bias1, gain2, w2, bias2, cache1, cache2):
    ids = jnp.stack([lax.axis_index(a) for a in ("core", "tm", "xh", "y")]).astype(jnp.int32)

    sent1, sent2, edges = run(
        send_kernel,
        [shape(8, 124, 128), shape(16, 128, 128), shape(96, 384)],
        [pltpu.VMEM((128, 128), F32), pltpu.VMEM((3, 448, 128), F32), pltpu.VMEM((96, 384), F32)],
        [ids, w1.transpose(1, 0, 2), w2.transpose(1, 0, 2), video, cache1, cache2],
        limit=60,
    )
    near2 = lax.all_to_all(sent2, ("y", "xh", "core"), 0, 0)
    edges, near2 = lax.optimization_barrier((edges, near2))
    halo = lax.ppermute(edges, LON, [(i, (i + 1) % 128 if i % 2 else (i - 1) % 128) for i in range(128)])
    slices, cache_own, vectors = run(
        own_kernel,
        [shape(4, 320, 128), shape(8, 16, 384), shape(8, 384, dtype=F32)],
        [pltpu.VMEM((3, 448, 128), F32), pltpu.VMEM((320, 384), F32)],
        [ids, video, cache1, cache2, gain1, bias1, gain2],
    )
    entering, cache_rows = run(
        enter_kernel,
        [shape(8, 400, 128), shape(9, 16, 384)],
        [],
        [ids, slices, cache_own, vectors, halo],
    )
    turned2 = run(turn_kernel, shape(128, 16, 128), [pltpu.VMEM((2048, 128), F32)], [near2], scalars=0)
    kernel2 = lax.all_gather(turned2, "z", axis=0, tiled=False)
    sent1, near2 = lax.optimization_barrier((sent1, near2))
    near1 = lax.all_to_all(sent1, "z", 0, 0)
    kernel1 = [near1] + [lax.ppermute(near1, "y", [(i, (i + d) % 4) for i in range(4)]) for d in (1, 2, 3)]
    entering, near1 = lax.optimization_barrier((entering, near1))
    entered = lax.all_to_all(entering, RING, 0, 0)
    part_own, part_peer = run(
        first_kernel,
        [shape(4, 14, 48, 128), shape(4, 14, 48, 128)],
        [
            pltpu.VMEM((36, 10, 8, 128), F32),
            pltpu.VMEM((3, 36, 80, 128), BF16),
            pltpu.VMEM((3, 36, 64, 128), BF16),
            pltpu.VMEM((4096, 128), F32),
            pltpu.VMEM((27, 128, 256), BF16),
            pltpu.VMEM((34, 64, 128), F32),
            pltpu.VMEM((34, 64, 128), F32),
        ],
        [ids, entered, *kernel1],
        flops=2 * 2176 * 27 * 128 * 256,
    )
    part_peer = lax.ppermute(part_peer, "core", [(0, 1), (1, 0)])
    parts = run(add_kernel, [shape(14, 48, 128)] * 4, [], [ids, part_own, part_peer])
    summands = [parts[0]] + [
        lax.ppermute(parts[n], ("xh", "tm"), [(i, i ^ n) for i in range(4)]) for n in (1, 2, 3)
    ]
    second = run(middle_kernel, shape(9, 48, 384), [], [ids, *summands, vectors, cache_rows])
    pair = lax.all_gather(second, "core", axis=0, tiled=True)
    own, peer = run(
        second_kernel,
        [shape(256, 256, dtype=F32), shape(256, 256, dtype=F32)],
        [
            pltpu.VMEM((3, 18, 48, 384), BF16),
            pltpu.VMEM((3, 18, 32, 384), BF16),
            pltpu.VMEM((512, 256), F32),
            pltpu.VMEM((512, 256), F32),
        ],
        [ids, pair, kernel2, bias2],
        flops=2 * 512 * 27 * 384 * 256,
    )
    peer = lax.ppermute(peer, "core", [(0, 1), (1, 0)])
    return run(last_kernel, shape(4, 8, 8, 384), [pltpu.VMEM((3, 256, 128), F32)], [ids, own, peer, video])


def solution(mesh):
    ring = Mesh(mesh.devices.reshape(4, 8, 2, 2, 2), (*LON, "tm"))
    field = P("tm", None, LON, None)
    cache = P(None, None, LON, None)
    kernel = P(None, LON, None)
    return jax.shard_map(
        per_device,
        mesh=ring,
        in_specs=(field, P(), kernel, P(), P(), kernel, P(), cache, cache),
        out_specs=field,
        check_vma=False,
    )
```

```python
import functools

import jax
import jax.numpy as jnp
from jax import lax
from jax.experimental import pallas as pl
from jax.experimental.pallas import tpu as pltpu
from jax.sharding import Mesh
from jax.sharding import PartitionSpec as P

LON = ("y", "z", "xh", "core")
RING = ("xh", "core", "tm")
PLANE = ("y", "z")
SWAP = [(0, 1), (1, 0)]
F32 = jnp.float32
BF16 = jnp.bfloat16
MIB = 1 << 20


def position():
    return [lax.axis_index(a) for a in ("core", "tm", "xh", "y")]


def lanes(shape):
    return lax.broadcasted_iota(jnp.int32, shape, len(shape) - 1)


def half_roll(x):
    return pltpu.roll(x, 64, x.ndim - 1)


def norm_silu(x, gain):
    square = jnp.mean(x * x, axis=-1, keepdims=True)
    scaled = x * lax.rsqrt(square + 1e-06) * gain
    return scaled / (1.0 + jnp.exp(-scaled))


def put(wide, at, value):
    for k in range(3):
        wide[k, at : at + value.shape[0]] = value[:, 128 * k : 128 * k + 128]


def every(wide, start, step):
    return jnp.concatenate([wide[k, pl.ds(start, 8, stride=step), :] for k in range(3)], axis=1)


def spread_matrix():
    row = lax.broadcasted_iota(jnp.int32, (384, 512), 0)
    k = lax.broadcasted_iota(jnp.int32, (384, 512), 1)
    q, r, yz = k >> 7, (k >> 5) & 3, k & 31
    return jnp.where((row == 12 * yz + 3 * q + r) & (r < 3), 1.0, 0.0)


def order_matrix():
    row = lax.broadcasted_iota(jnp.int32, (384, 384), 0)
    k = lax.broadcasted_iota(jnp.int32, (384, 384), 1)
    r, z, y, q = k >> 7, (k >> 4) & 7, (k >> 2) & 3, k & 3
    return jnp.where(row == 96 * y + 12 * z + 3 * q + r, 1.0, 0.0)


def pack(slot, taps, half):
    first = half == 0
    low_lanes = lanes((14, 128)) < 64
    for r, w in enumerate(taps):
        slot[pl.ds(r, 27, stride=3), :] = jnp.where(first, w[:, :128], w[:, 128:256])
        rest = w[:, 256:]
        turned = half_roll(rest)
        low = jnp.where(first, rest, turned)[:14]
        high = jnp.concatenate([jnp.where(first, turned, rest)[14:], jnp.zeros((1, 128), F32)], axis=0)
        slot[pl.ds(81 + r, 14, stride=3), :] = jnp.where(low_lanes, low, high)
    slot[123:] = jnp.zeros((5, 128), F32)


def by_slice(x, gain):
    frame = lax.rem(lax.broadcasted_iota(jnp.int32, x.shape, 0) >> 3, 5)
    x = jnp.where(frame == 4, x, norm_silu(x, gain)).astype(BF16)
    return jnp.dot(x, spread_matrix().astype(BF16), preferred_element_type=F32).astype(BF16)


def ordered(x):
    return jnp.dot(x.astype(BF16), order_matrix().astype(BF16), preferred_element_type=F32).astype(BF16)


def pack_kernel(w2, video, cache1, cache2, mine, peer, out_edge, slot, wide, edge):
    ids = position()
    taps = [w2[r].astype(F32) for r in range(3)]
    for half, out in ((ids[0], mine), (1 - ids[0], peer)):
        pack(slot, taps, half)
        out[...] = slot[:124].astype(BF16)
    upper = ids[0] == 1
    put(wide, 0, video[...].astype(F32).reshape(256, 384))
    put(wide, 256, cache1[ids[1]].astype(F32).reshape(64, 384))
    put(wide, 320, cache2[...].astype(F32).reshape(128, 384))

    def column(f, low, high):
        return jnp.where(upper, every(wide, 64 * f + high, 8), every(wide, 64 * f + low, 8))

    for c in range(2):
        for f in range(5):
            at = 40 * c + 8 * f
            edge[at : at + 8] = column(f, c, 6 + c)
    for f in range(2):
        edge[80 + 8 * f : 88 + 8 * f] = column(5 + f, 0, 7)
    out_edge[...] = edge[...].astype(BF16)


def send_kernel(
    w1, video, cache1, cache2, gain1, bias1, gain2,
    out1, out, out_cache, out_vec,
    slot, wide, rows,
):
    ids = position()
    order = order_matrix().astype(BF16)
    taps1 = [jnp.dot(w1[r], order, preferred_element_type=F32) for r in range(3)]
    pack(slot, taps1, ids[1])
    packed = slot[:124].astype(BF16)
    for n in range(8):
        out1[n] = packed

    put(wide, 0, video[...].astype(F32).reshape(256, 384))
    put(wide, 256, cache1[ids[1]].astype(F32).reshape(64, 384))
    put(wide, 320, cache2[...].astype(F32).reshape(128, 384))
    for c in range(8):
        for f in range(5):
            at = 40 * c + 8 * f
            rows[at : at + 8] = every(wide, 64 * f + c, 8)
    slices = by_slice(rows[...], gain1[...].reshape(1, 384))
    for q in range(4):
        out[q] = slices[:, 128 * q : 128 * q + 128]
    for c in range(8):
        for f in range(2):
            at = 16 * c + 8 * f
            rows[at : at + 8] = every(wide, 320 + 64 * f + c, 8)
    out_cache[...] = ordered(rows[0:128]).reshape(8, 16, 384)
    vectors = jnp.concatenate(
        [bias1[...].reshape(1, 384), gain2[...].reshape(1, 384), gain1[...].reshape(1, 384), jnp.zeros((5, 384), F32)],
        axis=0,
    )
    placed = jnp.dot(vectors, order_matrix(), preferred_element_type=F32, precision=lax.Precision.HIGHEST)
    out_vec[...] = jnp.concatenate([placed[:2], vectors[2:]], axis=0)


def join_kernel(axis, mine, other, out):
    at = position()[axis]
    out[at] = mine[...]
    out[1 - at] = other[...]


def turn_kernel(w0, w1, w2, w3, out, wide):
    y = position()[3]
    for d, w in enumerate((w0, w1, w2, w3)):
        at = pl.multiple_of(512 * ((y + 4 - d) & 3), 512)
        for n in range(4):
            wide[pl.ds(at + 128 * n, 124), :] = w[n].astype(F32)

    def step(row, carry):
        out[row] = wide[pl.ds(row, 16, stride=128), :].astype(BF16)
        return carry

    lax.fori_loop(0, 124, step, 0, unroll=4)


def enter_kernel(own, cache, vec, halo, keep, give, out_cache, edge):
    ids = position()
    slices = by_slice(halo[0:80].astype(F32), vec[2:3])
    for q in range(4):
        edge[q] = slices[:, 128 * q : 128 * q + 128]
    for xh in range(2):
        for out, core in ((keep, ids[0]), (give, 1 - ids[0])):
            out[xh, 0:320] = own[2 * xh + core]
            out[xh, 320:400] = edge[2 * xh + core]
    beyond = ordered(halo[80:96])

    @pl.when(ids[0] == 0)
    def _():
        out_cache[0] = beyond
        out_cache[1:9] = cache[...]

    @pl.when(ids[0] == 1)
    def _():
        out_cache[0:8] = cache[...]
        out_cache[8] = beyond


def arrange_kernel(keep, got, same, across):
    ids = position()
    same[0] = keep[ids[2]]
    same[1] = got[ids[2]]
    across[0] = keep[1 - ids[2]]
    across[1] = got[1 - ids[2]]


def shifted_rows(x, p):
    if p == 1:
        return x
    axis = x.ndim - 2
    lat = lax.broadcasted_iota(jnp.int32, x.shape, axis)
    if p == 0:
        return jnp.where(lat == 0, 0.0, pltpu.roll(x, 1, axis))
    return jnp.where(lat == 7, 0.0, pltpu.roll(x, 7, axis))


def tap_of(t):
    return t // 9, (t // 3) % 3, t % 3


def first_kernel(x0, x1, x2, x3, w0, w1, w2, w3, out_own, out_peer, field, even, odd, wide, kernel, part_a, part_b):
    ids = position()
    for n, x in enumerate((x0, x1, x2, x3)):
        tm = ids[1] ^ (n & 1)
        for m in range(2):
            q = 2 * (ids[2] ^ (n >> 1)) + (ids[0] ^ m)
            piece = x[m].astype(F32).reshape(10, 5, 8, 128)

            def place(at, begin, end):
                field[pl.ds(at, end - begin), pl.ds(2 + 4 * tm, 4)] = piece[begin:end, 0:4]
                field[pl.ds(at, end - begin), tm] = piece[begin:end, 4]

            place(2 + 8 * q, 0, 8)
            pl.when(q == 0)(lambda: place(0, 8, 10))
            pl.when(q == 3)(lambda: place(34, 8, 10))

    def spread(c, carry):
        plane = field[c]
        for p in range(3):
            moved = shifted_rows(plane, p)
            even[p, c] = moved.reshape(80, 128).astype(BF16)
            odd[p, c] = moved[1:9].reshape(64, 128).astype(BF16)
        return carry

    lax.fori_loop(0, 36, spread, 0, unroll=4)

    for d, w in enumerate((w0, w1, w2, w3)):
        at = pl.multiple_of(1024 * ((ids[3] + 4 - d) & 3), 1024)
        for z in range(8):
            wide[pl.ds(at + 128 * z, 124), :] = w[z].astype(F32)
    for t in range(27):
        for r in range(3):
            kernel[t, 32 * r : 32 * r + 32, 0:128] = wide[pl.ds(3 * t + r, 32, stride=128), :].astype(BF16)
            kernel[t, 32 * r : 32 * r + 32, 128:256] = wide[
                pl.ds(81 + 3 * (t % 14) + r, 32, stride=128), :
            ].astype(BF16)
        kernel[t, 96:128] = jnp.zeros((32, 256), BF16)

    block = 34

    def multiply(i, carry):
        at = i * block

        def window(t):
            a, p, q = tap_of(t)
            if a == 1:
                rows = odd[p, pl.ds(at + q, block)]
            else:
                rows = even[p, pl.ds(at + q, block), 8 * a : 8 * a + 64]
            return rows.reshape(block * 64, 128)

        def total(taps):
            left = jnp.concatenate([window(t) for t in taps], axis=1)
            right = kernel[taps[0] : taps[-1] + 1].reshape(128 * len(taps), 256)
            return jnp.dot(left, right, preferred_element_type=F32)

        low = total(range(0, 14))
        high = total(range(14, 27))
        part_a[pl.ds(at, block)] = (low[:, :128] + high[:, :128]).reshape(block, 64, 128)
        part_b[pl.ds(at, block)] = (low[:, 128:] + half_roll(high[:, 128:])).reshape(block, 64, 128)
        return carry

    lax.fori_loop(0, 34 // block, multiply, 0)

    low_lanes = lanes((48, 128)) < 64
    for d in range(4):
        xh, tm = d // 2, d % 2
        for out, core in ((out_own, ids[0]), (out_peer, 1 - ids[0])):
            base = 16 * xh + 9 * core

            def rows_of(part, c):
                if tm == 1:
                    return part[c, 16:64]
                return jnp.concatenate([jnp.zeros((16, 128), F32), part[c, 0:32]], axis=0)

            for j in range(9):
                out[d, j] = rows_of(part_a, base + j).astype(BF16)
            for j in range(5):
                b = rows_of(part_b, base + j)
                if j < 4:
                    b = jnp.where(low_lanes, b, half_roll(rows_of(part_b, base + j + 5)))
                out[d, 9 + j] = b.astype(BF16)


def add_kernel(x, y, *outs):
    ids = position()
    for n, out in enumerate(outs):
        d = 2 * (ids[2] ^ (n >> 1)) + (ids[1] ^ (n & 1))

        def step(j, carry):
            out[j] = (x[d, j].astype(F32) + y[d, j].astype(F32)).astype(BF16)
            return carry

        lax.fori_loop(0, 14, step, 0, unroll=2)


def middle_kernel(x0, x1, x2, x3, vec, cache, out):
    ids = position()
    low_lanes = lanes((48, 128)) < 64
    starts = ids[1] == 0
    bias, gain = vec[0:1], vec[1:2]

    def summed(tm, j):
        mine = x0[j].astype(F32) + x2[j].astype(F32)
        other = x1[j].astype(F32) + x3[j].astype(F32)
        return jnp.where(ids[1] == tm, mine, other)

    for j in range(5):
        b0, b1 = summed(0, 9 + j), summed(1, 9 + j)
        places = [(j, jnp.where(low_lanes, b0, half_roll(b1)))]
        if j < 4:
            places.append((j + 5, jnp.where(low_lanes, half_roll(b0), b1)))
        for c, b in places:
            hidden = jnp.concatenate([summed(0, c), summed(1, c), b], axis=1) + bias
            normed = norm_silu(hidden, gain).astype(BF16)
            out[c, 16:48] = normed[16:48]
            out[c, 0:16] = jnp.where(starts, cache[c], normed[0:16])


def second_kernel(mine, other, w, bias, out_own, out_peer, even, odd, low, high):
    ids = position()
    def spread(c, carry):
        for x, core in ((mine, ids[0]), (other, 1 - ids[0])):
            plane = x[c].astype(F32).reshape(6, 8, 384)
            at = 9 * core + c
            for p in range(3):
                moved = shifted_rows(plane, p)
                even[p, at] = moved.reshape(48, 384).astype(BF16)
                odd[p, at] = moved[1:5].reshape(32, 384).astype(BF16)
        return carry

    lax.fori_loop(0, 9, spread, 0)

    def window(t):
        a, p, q = tap_of(t)
        if a == 1:
            rows = odd[p, q : q + 16]
        else:
            rows = even[p, q : q + 16, 8 * a : 8 * a + 32]
        return rows.reshape(512, 384)

    def kernel(t):
        a = [w[:, 3 * t + r].reshape(128, 128) for r in range(3)]
        b = [w[:, 81 + 3 * (t % 14) + r].reshape(128, 128) for r in range(3)]
        return jnp.concatenate([jnp.concatenate(a, axis=0), jnp.concatenate(b, axis=0)], axis=1)

    for begin, end, total in ((0, 14, low), (14, 27, high)):
        for t in range(begin, end, 2):
            taps = range(t, min(t + 2, end))
            left = jnp.concatenate([window(s) for s in taps], axis=1)
            right = jnp.concatenate([kernel(s) for s in taps], axis=0)
            product = jnp.dot(left, right, preferred_element_type=F32)
            if t == begin:
                total[...] = product
            else:
                total[...] += product

    first = ids[0] == 0
    bias = bias[...].reshape(1, 384)
    rest = bias[:, 256:]
    bias_a = jnp.where(first, bias[:, :128], bias[:, 128:256])
    bias_b = jnp.where(first, rest, half_roll(rest))
    low[:, :128] = low[:, :128] + high[:, :128] + bias_a
    low[:, 128:] = low[:, 128:] + half_roll(high[:, 128:]) + bias_b
    own = pl.multiple_of(256 * ids[0], 256)
    peer = pl.multiple_of(256 - 256 * ids[0], 256)
    out_own[...] = low[pl.ds(own, 256)]
    out_peer[...] = low[pl.ds(peer, 256)]


def last_kernel(own, peer, video, out, rows):
    ids = position()
    first = ids[0] == 0
    low_lanes = lanes((256, 128)) < 64
    rows[0] = jnp.where(first, own[:, :128], peer[:, :128])
    rows[1] = jnp.where(first, peer[:, :128], own[:, :128])
    b0 = jnp.where(first, own[:, 128:], peer[:, 128:])
    b1 = jnp.where(first, peer[:, 128:], own[:, 128:])
    rows[2] = jnp.where(low_lanes, b0, half_roll(b1))
    for f in range(4):
        for i in range(8):
            branch = every(rows, 8 * f + i, 32)
            out[f, i] = (video[f, i].astype(F32) + branch).astype(BF16)


def run(kernel, outs, scratch, args, flops=0, limit=48):
    specs = [pl.BlockSpec(memory_space=pltpu.VMEM)] * len(args)
    moved = sum(a.size * a.dtype.itemsize for a in args)
    return pl.pallas_call(
        kernel,
        out_shape=outs,
        in_specs=specs,
        out_specs=jax.tree.map(lambda _: pl.BlockSpec(memory_space=pltpu.VMEM), outs),
        scratch_shapes=scratch,
        compiler_params=pltpu.CompilerParams(vmem_limit_bytes=limit * MIB),
        cost_estimate=pl.CostEstimate(flops=flops, bytes_accessed=moved, transcendentals=0),
    )(*args)


def round_y(x):
    return [lax.ppermute(x, "y", [(i, (i + d) % 4) for i in range(4)]) for d in (1, 2, 3)]


def shape(*dims, dtype=BF16):
    return jax.ShapeDtypeStruct(dims, dtype)


def per_device(video, gain1, w1, bias1, gain2, w2, bias2, cache1, cache2):
    w1, w2 = w1.transpose(1, 0, 2), w2.transpose(1, 0, 2)
    mine2, peer2, edges = run(
        pack_kernel,
        [shape(124, 128), shape(124, 128), shape(96, 384)],
        [pltpu.VMEM((128, 128), F32), pltpu.VMEM((3, 448, 128), F32), pltpu.VMEM((96, 384), F32)],
        [w2, video, cache1, cache2],
        limit=60,
    )
    peer2 = lax.ppermute(peer2, "core", SWAP)
    pair2 = run(functools.partial(join_kernel, 0), shape(2, 124, 128), [], [mine2, peer2])
    pair2, w1 = lax.optimization_barrier((pair2, w1))
    sent1, slices, cache_own, vectors = run(
        send_kernel,
        [
            shape(8, 124, 128),
            shape(4, 320, 128),
            shape(8, 16, 384),
            shape(8, 384, dtype=F32),
        ],
        [
            pltpu.VMEM((128, 128), F32),
            pltpu.VMEM((3, 448, 128), F32),
            pltpu.VMEM((320, 384), F32),
        ],
        [w1, video, cache1, cache2, gain1, bias1, gain2],
        limit=60,
    )
    other2 = lax.ppermute(pair2, "xh", SWAP)
    quad2 = run(functools.partial(join_kernel, 2), shape(2, 2, 124, 128), [], [pair2, other2])
    quad2 = quad2.reshape(4, 124, 128)
    quad2, sent1 = lax.optimization_barrier((quad2, sent1))
    near2 = [quad2, *round_y(quad2)]
    halo = lax.ppermute(edges, LON, [(i, (i + 1) % 128 if i % 2 else (i - 1) % 128) for i in range(128)])
    turned2 = run(turn_kernel, shape(124, 16, 128), [pltpu.VMEM((2048, 128), F32)], near2)
    sent1, turned2, halo = lax.optimization_barrier((sent1, turned2, halo))
    near1 = lax.all_to_all(sent1, "z", 0, 0)
    kernel2 = lax.all_gather(turned2, "z", axis=0, tiled=False)
    keep, give, cache_rows = run(
        enter_kernel,
        [shape(2, 400, 128), shape(2, 400, 128), shape(9, 16, 384)],
        [pltpu.VMEM((4, 80, 128), BF16)],
        [slices, cache_own, vectors, halo],
    )
    got = lax.ppermute(give, "core", SWAP)
    same, across = run(arrange_kernel, [shape(2, 400, 128)] * 2, [], [keep, got])
    entered = [same] + [
        lax.ppermute(v, ("xh", "tm"), [(i, i ^ n) for i in range(4)]) for n, v in ((1, same), (2, across), (3, across))
    ]
    kernel1 = [near1, *round_y(near1)]
    part_own, part_peer = run(
        first_kernel,
        [shape(4, 14, 48, 128), shape(4, 14, 48, 128)],
        [
            pltpu.VMEM((36, 10, 8, 128), F32),
            pltpu.VMEM((3, 36, 80, 128), BF16),
            pltpu.VMEM((3, 36, 64, 128), BF16),
            pltpu.VMEM((4096, 128), F32),
            pltpu.VMEM((27, 128, 256), BF16),
            pltpu.VMEM((34, 64, 128), F32),
            pltpu.VMEM((34, 64, 128), F32),
        ],
        [*entered, *kernel1],
        flops=2 * 2176 * 27 * 128 * 256,
    )
    part_peer = lax.ppermute(part_peer, "core", SWAP)
    parts = run(add_kernel, [shape(14, 48, 128)] * 4, [], [part_own, part_peer])
    summands = [parts[0]] + [
        lax.ppermute(parts[n], ("xh", "tm"), [(i, i ^ n) for i in range(4)]) for n in (1, 2, 3)
    ]
    second = run(middle_kernel, shape(9, 48, 384), [], [*summands, vectors, cache_rows])
    second, kernel2 = lax.optimization_barrier((second, kernel2))
    other = lax.ppermute(second, "core", SWAP)
    own, peer = run(
        second_kernel,
        [shape(256, 256, dtype=F32), shape(256, 256, dtype=F32)],
        [
            pltpu.VMEM((3, 18, 48, 384), BF16),
            pltpu.VMEM((3, 18, 32, 384), BF16),
            pltpu.VMEM((512, 256), F32),
            pltpu.VMEM((512, 256), F32),
        ],
        [second, other, kernel2, bias2],
        flops=2 * 512 * 27 * 384 * 256,
    )
    peer = lax.ppermute(peer, "core", SWAP)
    return run(last_kernel, shape(4, 8, 8, 384), [pltpu.VMEM((3, 256, 128), F32)], [own, peer, video])


def solution(mesh):
    ring = Mesh(mesh.devices.reshape(4, 8, 2, 2, 2), (*LON, "tm"))
    field = P("tm", None, LON, None)
    cache = P(None, None, LON, None)
    kernel = P(None, LON, None)
    return jax.shard_map(
        per_device,
        mesh=ring,
        in_specs=(field, P(), kernel, P(), P(), kernel, P(), cache, cache),
        out_specs=field,
        check_vma=False,
    )
```

```python
import functools

import jax
import jax.numpy as jnp
from jax import lax
from jax.experimental import pallas as pl
from jax.experimental.pallas import tpu as pltpu
from jax.sharding import Mesh
from jax.sharding import PartitionSpec as P

LON = ("y", "z", "xh", "core")
RING = ("xh", "core", "tm")
PLANE = ("y", "z")
SWAP = [(0, 1), (1, 0)]
F32 = jnp.float32
BF16 = jnp.bfloat16
MIB = 1 << 20


def position():
    return [lax.axis_index(a) for a in ("core", "tm", "xh", "y")]


def lanes(shape):
    return lax.broadcasted_iota(jnp.int32, shape, len(shape) - 1)


def half_roll(x):
    return pltpu.roll(x, 64, x.ndim - 1)


def norm_silu(x, gain):
    square = jnp.mean(x * x, axis=-1, keepdims=True)
    scaled = x * lax.rsqrt(square + 1e-06) * gain
    return scaled / (1.0 + jnp.exp(-scaled))


def put(wide, at, value):
    for k in range(3):
        wide[k, at : at + value.shape[0]] = value[:, 128 * k : 128 * k + 128]


def every(wide, start, step):
    return jnp.concatenate([wide[k, pl.ds(start, 8, stride=step), :] for k in range(3)], axis=1)


def spread_matrix():
    row = lax.broadcasted_iota(jnp.int32, (384, 512), 0)
    k = lax.broadcasted_iota(jnp.int32, (384, 512), 1)
    q, r, yz = k >> 7, (k >> 5) & 3, k & 31
    return jnp.where((row == 12 * yz + 3 * q + r) & (r < 3), 1.0, 0.0)


def order_matrix():
    row = lax.broadcasted_iota(jnp.int32, (384, 384), 0)
    k = lax.broadcasted_iota(jnp.int32, (384, 384), 1)
    r, z, y, q = k >> 7, (k >> 4) & 7, (k >> 2) & 3, k & 3
    return jnp.where(row == 96 * y + 12 * z + 3 * q + r, 1.0, 0.0)


def pack(slot, taps, half):
    first = half == 0
    low_lanes = lanes((14, 128)) < 64
    for r, w in enumerate(taps):
        slot[pl.ds(r, 27, stride=3), :] = jnp.where(first, w[:, :128], w[:, 128:256])
        rest = w[:, 256:]
        turned = half_roll(rest)
        low = jnp.where(first, rest, turned)[:14]
        high = jnp.concatenate([jnp.where(first, turned, rest)[14:], jnp.zeros((1, 128), F32)], axis=0)
        slot[pl.ds(81 + r, 14, stride=3), :] = jnp.where(low_lanes, low, high)
    slot[123:] = jnp.zeros((5, 128), F32)


def by_slice(x, gain):
    frame = lax.rem(lax.broadcasted_iota(jnp.int32, x.shape, 0) >> 3, 5)
    x = jnp.where(frame == 4, x, norm_silu(x, gain)).astype(BF16)
    return jnp.dot(x, spread_matrix().astype(BF16), preferred_element_type=F32)


def squeezed(x):
    free = lanes((80, 128)) >= 96
    kept = [jnp.where(free, pltpu.roll(x[240:], 96 - 32 * k, 1), x[80 * k : 80 * k + 80]) for k in range(3)]
    return jnp.concatenate(kept, axis=0)


def stretched(x):
    lane = lanes((80, 128))
    parts = [x[80 * k : 80 * k + 80] for k in range(3)]
    last = jnp.zeros((80, 128), F32)
    for k in range(3):
        last = jnp.where(lane >> 5 == k, pltpu.roll(parts[k], 32 + 32 * k, 1), last)
    return jnp.concatenate([jnp.where(lane < 96, part, 0.0) for part in parts] + [last], axis=0)


def ordered(x):
    return jnp.dot(x.astype(BF16), order_matrix().astype(BF16), preferred_element_type=F32).astype(BF16)


def pack_kernel(w2, video, cache1, cache2, mine, peer, out_edge, slot, wide, edge):
    ids = position()
    taps = [w2[r].astype(F32) for r in range(3)]
    for half, out in ((ids[0], mine), (1 - ids[0], peer)):
        pack(slot, taps, half)
        out[...] = slot[:124].astype(BF16)
    upper = ids[0] == 1
    put(wide, 0, video[...].astype(F32).reshape(256, 384))
    put(wide, 256, cache1[ids[1]].astype(F32).reshape(64, 384))
    put(wide, 320, cache2[...].astype(F32).reshape(128, 384))

    def column(f, low, high):
        return jnp.where(upper, every(wide, 64 * f + high, 8), every(wide, 64 * f + low, 8))

    for c in range(2):
        for f in range(5):
            at = 40 * c + 8 * f
            edge[at : at + 8] = column(f, c, 6 + c)
    for f in range(2):
        edge[80 + 8 * f : 88 + 8 * f] = column(5 + f, 0, 7)
    out_edge[...] = edge[...].astype(BF16)


def send_kernel(
    w1, video, cache1, cache2, gain1, bias1, gain2,
    out1, out, out_cache, out_vec,
    slot, wide, rows,
):
    ids = position()
    order = order_matrix().astype(BF16)
    taps1 = [jnp.dot(w1[r], order, preferred_element_type=F32) for r in range(3)]
    pack(slot, taps1, ids[1])
    packed = slot[:124].astype(BF16)
    for n in range(8):
        out1[n] = packed

    put(wide, 0, video[...].astype(F32).reshape(256, 384))
    put(wide, 256, cache1[ids[1]].astype(F32).reshape(64, 384))
    put(wide, 320, cache2[...].astype(F32).reshape(128, 384))
    for c in range(8):
        for f in range(5):
            at = 40 * c + 8 * f
            rows[at : at + 8] = every(wide, 64 * f + c, 8)
    slices = by_slice(rows[...], gain1[...].reshape(1, 384))
    for q in range(4):
        out[q] = squeezed(slices[:, 128 * q : 128 * q + 128]).astype(BF16)
    for c in range(8):
        for f in range(2):
            at = 16 * c + 8 * f
            rows[at : at + 8] = every(wide, 320 + 64 * f + c, 8)
    out_cache[...] = ordered(rows[0:128]).reshape(8, 16, 384)
    vectors = jnp.concatenate(
        [bias1[...].reshape(1, 384), gain2[...].reshape(1, 384), gain1[...].reshape(1, 384), jnp.zeros((5, 384), F32)],
        axis=0,
    )
    placed = jnp.dot(vectors, order_matrix(), preferred_element_type=F32, precision=lax.Precision.HIGHEST)
    out_vec[...] = jnp.concatenate([placed[:2], vectors[2:]], axis=0)


def join_kernel(axis, mine, other, out):
    at = position()[axis]
    out[at] = mine[...]
    out[1 - at] = other[...]


def turn_kernel(w0, w1, w2, w3, out, wide):
    y = position()[3]
    for d, w in enumerate((w0, w1, w2, w3)):
        at = pl.multiple_of(512 * ((y + 4 - d) & 3), 512)
        for n in range(4):
            wide[pl.ds(at + 128 * n, 124), :] = w[n].astype(F32)

    def step(row, carry):
        out[row] = wide[pl.ds(row, 16, stride=128), :].astype(BF16)
        return carry

    lax.fori_loop(0, 124, step, 0, unroll=4)


def enter_kernel(own, gain, halo, keep, give, out_cache, edge):
    ids = position()
    slices = by_slice(halo[0:80].astype(F32), gain[...].reshape(1, 384))
    for q in range(4):
        edge[q] = slices[:, 128 * q : 128 * q + 128].astype(BF16)
    for xh in range(2):
        for out, core in ((keep, ids[0]), (give, 1 - ids[0])):
            out[xh, 0:240] = own[2 * xh + core]
            out[xh, 240:320] = edge[2 * xh + core]
    out_cache[...] = ordered(halo[80:96])


def arrange_kernel(keep, got, same, across):
    ids = position()
    same[0] = keep[ids[2]]
    same[1] = got[ids[2]]
    across[0] = keep[1 - ids[2]]
    across[1] = got[1 - ids[2]]


def shifted_rows(x, p):
    if p == 1:
        return x
    axis = x.ndim - 2
    lat = lax.broadcasted_iota(jnp.int32, x.shape, axis)
    if p == 0:
        return jnp.where(lat == 0, 0.0, pltpu.roll(x, 1, axis))
    return jnp.where(lat == 7, 0.0, pltpu.roll(x, 7, axis))


def tap_of(t):
    return t // 9, (t // 3) % 3, t % 3


def field_kernel(x0, x1, x2, x3, even, odd, field):
    ids = position()
    for n, x in enumerate((x0, x1, x2, x3)):
        tm = ids[1] ^ (n & 1)
        for m in range(2):
            q = 2 * (ids[2] ^ (n >> 1)) + (ids[0] ^ m)
            packed = x[m].astype(F32)
            piece = jnp.concatenate([stretched(packed[:240]), packed[240:]], axis=0).reshape(10, 5, 8, 128)

            def place(at, begin, end):
                field[pl.ds(at, end - begin), pl.ds(2 + 4 * tm, 4)] = piece[begin:end, 0:4]
                field[pl.ds(at, end - begin), tm] = piece[begin:end, 4]

            place(2 + 8 * q, 0, 8)
            pl.when(q == 0)(lambda: place(0, 8, 10))
            pl.when(q == 3)(lambda: place(34, 8, 10))

    def spread(c, carry):
        plane = field[c]
        for p in range(3):
            moved = shifted_rows(plane, p)
            even[p, c] = moved.reshape(80, 128).astype(BF16)
            odd[p, c] = moved[1:9].reshape(64, 128).astype(BF16)
        return carry

    lax.fori_loop(0, 36, spread, 0, unroll=4)


def first_kernel(even, odd, w0, w1, w2, w3, out_own, out_peer, wide, kernel, part_a, part_b):
    ids = position()
    for d, w in enumerate((w0, w1, w2, w3)):
        at = pl.multiple_of(1024 * ((ids[3] + 4 - d) & 3), 1024)
        for z in range(8):
            wide[pl.ds(at + 128 * z, 124), :] = w[z].astype(F32)
    for t in range(27):
        for r in range(3):
            kernel[t, 32 * r : 32 * r + 32, 0:128] = wide[pl.ds(3 * t + r, 32, stride=128), :].astype(BF16)
            kernel[t, 32 * r : 32 * r + 32, 128:256] = wide[
                pl.ds(81 + 3 * (t % 14) + r, 32, stride=128), :
            ].astype(BF16)
        kernel[t, 96:128] = jnp.zeros((32, 256), BF16)

    block = 34

    def multiply(i, carry):
        at = i * block

        def window(t):
            a, p, q = tap_of(t)
            if a == 1:
                rows = odd[p, pl.ds(at + q, block)]
            else:
                rows = even[p, pl.ds(at + q, block), 8 * a : 8 * a + 64]
            return rows.reshape(block * 64, 128)

        def total(taps):
            left = jnp.concatenate([window(t) for t in taps], axis=1)
            right = kernel[taps[0] : taps[-1] + 1].reshape(128 * len(taps), 256)
            return jnp.dot(left, right, preferred_element_type=F32)

        low = total(range(0, 14))
        high = total(range(14, 27))
        part_a[pl.ds(at, block)] = (low[:, :128] + high[:, :128]).reshape(block, 64, 128)
        part_b[pl.ds(at, block)] = (low[:, 128:] + half_roll(high[:, 128:])).reshape(block, 64, 128)
        return carry

    lax.fori_loop(0, 34 // block, multiply, 0)

    low_lanes = lanes((48, 128)) < 64
    for d in range(4):
        xh, tm = d // 2, d % 2
        for out, core in ((out_own, ids[0]), (out_peer, 1 - ids[0])):
            base = 16 * xh + 9 * core

            def rows_of(part, c):
                if tm == 1:
                    return part[c, 16:64]
                return jnp.concatenate([jnp.zeros((16, 128), F32), part[c, 0:32]], axis=0)

            for j in range(9):
                out[d, j] = rows_of(part_a, base + j).astype(BF16)
            for j in range(5):
                b = rows_of(part_b, base + j)
                if j < 4:
                    b = jnp.where(low_lanes, b, half_roll(rows_of(part_b, base + j + 5)))
                out[d, 9 + j] = b.astype(BF16)


def add_kernel(x, y, *outs):
    ids = position()
    for n, out in enumerate(outs):
        d = 2 * (ids[2] ^ (n >> 1)) + (ids[1] ^ (n & 1))

        def step(j, carry):
            out[j] = (x[d, j].astype(F32) + y[d, j].astype(F32)).astype(BF16)
            return carry

        lax.fori_loop(0, 14, step, 0, unroll=2)


def middle_kernel(x0, x1, x2, x3, vec, cache, beyond, out):
    ids = position()
    low_lanes = lanes((48, 128)) < 64
    starts = ids[1] == 0

    def cached(c):
        low = beyond[...] if c == 0 else cache[c - 1]
        high = beyond[...] if c == 8 else cache[c]
        return jnp.where(ids[0] == 0, low, high)

    bias, gain = vec[0:1], vec[1:2]

    def summed(tm, j):
        mine = x0[j].astype(F32) + x2[j].astype(F32)
        other = x1[j].astype(F32) + x3[j].astype(F32)
        return jnp.where(ids[1] == tm, mine, other)

    for j in range(5):
        b0, b1 = summed(0, 9 + j), summed(1, 9 + j)
        places = [(j, jnp.where(low_lanes, b0, half_roll(b1)))]
        if j < 4:
            places.append((j + 5, jnp.where(low_lanes, half_roll(b0), b1)))
        for c, b in places:
            hidden = jnp.concatenate([summed(0, c), summed(1, c), b], axis=1) + bias
            normed = norm_silu(hidden, gain).astype(BF16)
            out[c, 16:48] = normed[16:48]
            out[c, 0:16] = jnp.where(starts, cached(c), normed[0:16])


def second_kernel(mine, other, w, bias, out_own, out_peer, even, odd, low, high):
    ids = position()
    def spread(c, carry):
        for x, core in ((mine, ids[0]), (other, 1 - ids[0])):
            plane = x[c].astype(F32).reshape(6, 8, 384)
            at = 9 * core + c
            for p in range(3):
                moved = shifted_rows(plane, p)
                even[p, at] = moved.reshape(48, 384).astype(BF16)
                odd[p, at] = moved[1:5].reshape(32, 384).astype(BF16)
        return carry

    lax.fori_loop(0, 9, spread, 0)

    def window(t):
        a, p, q = tap_of(t)
        if a == 1:
            rows = odd[p, q : q + 16]
        else:
            rows = even[p, q : q + 16, 8 * a : 8 * a + 32]
        return rows.reshape(512, 384)

    def kernel(t):
        a = [w[:, 3 * t + r].reshape(128, 128) for r in range(3)]
        b = [w[:, 81 + 3 * (t % 14) + r].reshape(128, 128) for r in range(3)]
        return jnp.concatenate([jnp.concatenate(a, axis=0), jnp.concatenate(b, axis=0)], axis=1)

    for begin, end, total in ((0, 14, low), (14, 27, high)):
        for t in range(begin, end, 2):
            taps = range(t, min(t + 2, end))
            left = jnp.concatenate([window(s) for s in taps], axis=1)
            right = jnp.concatenate([kernel(s) for s in taps], axis=0)
            product = jnp.dot(left, right, preferred_element_type=F32)
            if t == begin:
                total[...] = product
            else:
                total[...] += product

    first = ids[0] == 0
    bias = bias[...].reshape(1, 384)
    rest = bias[:, 256:]
    bias_a = jnp.where(first, bias[:, :128], bias[:, 128:256])
    bias_b = jnp.where(first, rest, half_roll(rest))
    low[:, :128] = low[:, :128] + high[:, :128] + bias_a
    low[:, 128:] = low[:, 128:] + half_roll(high[:, 128:]) + bias_b
    own = pl.multiple_of(256 * ids[0], 256)
    peer = pl.multiple_of(256 - 256 * ids[0], 256)
    out_own[...] = low[pl.ds(own, 256)]
    out_peer[...] = low[pl.ds(peer, 256)]


def last_kernel(own, peer, video, out, rows):
    ids = position()
    first = ids[0] == 0
    low_lanes = lanes((256, 128)) < 64
    rows[0] = jnp.where(first, own[:, :128], peer[:, :128])
    rows[1] = jnp.where(first, peer[:, :128], own[:, :128])
    b0 = jnp.where(first, own[:, 128:], peer[:, 128:])
    b1 = jnp.where(first, peer[:, 128:], own[:, 128:])
    rows[2] = jnp.where(low_lanes, b0, half_roll(b1))
    for f in range(4):
        for i in range(8):
            branch = every(rows, 8 * f + i, 32)
            out[f, i] = (video[f, i].astype(F32) + branch).astype(BF16)


def run(kernel, outs, scratch, args, flops=0, limit=48):
    specs = [pl.BlockSpec(memory_space=pltpu.VMEM)] * len(args)
    moved = sum(a.size * a.dtype.itemsize for a in args)
    return pl.pallas_call(
        kernel,
        out_shape=outs,
        in_specs=specs,
        out_specs=jax.tree.map(lambda _: pl.BlockSpec(memory_space=pltpu.VMEM), outs),
        scratch_shapes=scratch,
        compiler_params=pltpu.CompilerParams(vmem_limit_bytes=limit * MIB),
        cost_estimate=pl.CostEstimate(flops=flops, bytes_accessed=moved, transcendentals=0),
    )(*args)


def round_y(x):
    return [lax.ppermute(x, "y", [(i, (i + d) % 4) for i in range(4)]) for d in (1, 2, 3)]


def shape(*dims, dtype=BF16):
    return jax.ShapeDtypeStruct(dims, dtype)


def per_device(video, gain1, w1, bias1, gain2, w2, bias2, cache1, cache2):
    w1, w2 = w1.transpose(1, 0, 2), w2.transpose(1, 0, 2)
    mine2, peer2, edges = run(
        pack_kernel,
        [shape(124, 128), shape(124, 128), shape(96, 384)],
        [pltpu.VMEM((128, 128), F32), pltpu.VMEM((3, 448, 128), F32), pltpu.VMEM((96, 384), F32)],
        [w2, video, cache1, cache2],
        limit=60,
    )
    peer2 = lax.ppermute(peer2, "core", SWAP)
    pair2 = run(functools.partial(join_kernel, 0), shape(2, 124, 128), [], [mine2, peer2])
    pair2, w1 = lax.optimization_barrier((pair2, w1))
    sent1, slices, cache_own, vectors = run(
        send_kernel,
        [
            shape(8, 124, 128),
            shape(4, 240, 128),
            shape(8, 16, 384),
            shape(8, 384, dtype=F32),
        ],
        [
            pltpu.VMEM((128, 128), F32),
            pltpu.VMEM((3, 448, 128), F32),
            pltpu.VMEM((320, 384), F32),
        ],
        [w1, video, cache1, cache2, gain1, bias1, gain2],
        limit=60,
    )
    other2 = lax.ppermute(pair2, "xh", SWAP)
    quad2 = run(functools.partial(join_kernel, 2), shape(2, 2, 124, 128), [], [pair2, other2])
    quad2 = quad2.reshape(4, 124, 128)
    quad2, sent1 = lax.optimization_barrier((quad2, sent1))
    near2 = [quad2, *round_y(quad2)]
    halo = lax.ppermute(edges, LON, [(i, (i + 1) % 128 if i % 2 else (i - 1) % 128) for i in range(128)])
    turned2 = run(turn_kernel, shape(124, 16, 128), [pltpu.VMEM((2048, 128), F32)], near2)
    sent1, turned2, halo = lax.optimization_barrier((sent1, turned2, halo))
    near1 = lax.all_to_all(sent1, "z", 0, 0)
    kernel2 = lax.all_gather(turned2, "z", axis=0, tiled=False)
    keep, give, beyond = run(
        enter_kernel,
        [shape(2, 320, 128), shape(2, 320, 128), shape(16, 384)],
        [pltpu.VMEM((4, 80, 128), BF16)],
        [slices, gain1, halo],
    )
    got = lax.ppermute(give, "core", SWAP)
    same, across = run(arrange_kernel, [shape(2, 320, 128)] * 2, [], [keep, got])
    entered = [same] + [
        lax.ppermute(v, ("xh", "tm"), [(i, i ^ n) for i in range(4)]) for n, v in ((1, same), (2, across), (3, across))
    ]
    kernel1 = [near1, *round_y(near1)]
    even, odd = run(
        field_kernel,
        [shape(3, 36, 80, 128), shape(3, 36, 64, 128)],
        [pltpu.VMEM((36, 10, 8, 128), F32)],
        entered,
        limit=40,
    )
    part_own, part_peer = run(
        first_kernel,
        [shape(4, 14, 48, 128), shape(4, 14, 48, 128)],
        [
            pltpu.VMEM((4096, 128), F32),
            pltpu.VMEM((27, 128, 256), BF16),
            pltpu.VMEM((34, 64, 128), F32),
            pltpu.VMEM((34, 64, 128), F32),
        ],
        [even, odd, *kernel1],
        flops=2 * 2176 * 27 * 128 * 256,
        limit=40,
    )
    part_peer = lax.ppermute(part_peer, "core", SWAP)
    parts = run(add_kernel, [shape(14, 48, 128)] * 4, [], [part_own, part_peer])
    summands = [parts[0]] + [
        lax.ppermute(parts[n], ("xh", "tm"), [(i, i ^ n) for i in range(4)]) for n in (1, 2, 3)
    ]
    second = run(middle_kernel, shape(9, 48, 384), [], [*summands, vectors, cache_own, beyond])
    other = lax.ppermute(second, "core", SWAP)
    own, peer = run(
        second_kernel,
        [shape(256, 256, dtype=F32), shape(256, 256, dtype=F32)],
        [
            pltpu.VMEM((3, 18, 48, 384), BF16),
            pltpu.VMEM((3, 18, 32, 384), BF16),
            pltpu.VMEM((512, 256), F32),
            pltpu.VMEM((512, 256), F32),
        ],
        [second, other, kernel2, bias2],
        flops=2 * 512 * 27 * 384 * 256,
    )
    peer = lax.ppermute(peer, "core", SWAP)
    return run(last_kernel, shape(4, 8, 8, 384), [pltpu.VMEM((3, 256, 128), F32)], [own, peer, video])


def solution(mesh):
    ring = Mesh(mesh.devices.reshape(4, 8, 2, 2, 2), (*LON, "tm"))
    field = P("tm", None, LON, None)
    cache = P(None, None, LON, None)
    kernel = P(None, LON, None)
    return jax.shard_map(
        per_device,
        mesh=ring,
        in_specs=(field, P(), kernel, P(), P(), kernel, P(), cache, cache),
        out_specs=field,
        check_vma=False,
    )
```

```python
import functools

import jax
import jax.numpy as jnp
from jax import lax
from jax.experimental import pallas as pl
from jax.experimental.pallas import tpu as pltpu
from jax.sharding import Mesh
from jax.sharding import PartitionSpec as P

LON = ("y", "z", "xh", "core")
RING = ("xh", "core", "tm")
PLANE = ("y", "z")
SWAP = [(0, 1), (1, 0)]
F32 = jnp.float32
BF16 = jnp.bfloat16
MIB = 1 << 20


def position():
    return [lax.axis_index(a) for a in ("core", "tm", "xh", "y")]


def lanes(shape):
    return lax.broadcasted_iota(jnp.int32, shape, len(shape) - 1)


def half_roll(x):
    return pltpu.roll(x, 64, x.ndim - 1)


def norm_silu(x, gain):
    square = jnp.mean(x * x, axis=-1, keepdims=True)
    scaled = x * lax.rsqrt(square + 1e-06) * gain
    return scaled / (1.0 + jnp.exp(-scaled))


def put(wide, at, value):
    for k in range(3):
        wide[k, at : at + value.shape[0]] = value[:, 128 * k : 128 * k + 128]


def every(wide, start, step):
    return jnp.concatenate([wide[k, pl.ds(start, 8, stride=step), :] for k in range(3)], axis=1)


def spread_matrix():
    row = lax.broadcasted_iota(jnp.int32, (384, 512), 0)
    k = lax.broadcasted_iota(jnp.int32, (384, 512), 1)
    q, r, yz = k >> 7, (k >> 5) & 3, k & 31
    return jnp.where((row == 12 * yz + 3 * q + r) & (r < 3), 1.0, 0.0)


def order_matrix():
    row = lax.broadcasted_iota(jnp.int32, (384, 384), 0)
    k = lax.broadcasted_iota(jnp.int32, (384, 384), 1)
    r, z, y, q = k >> 7, (k >> 4) & 7, (k >> 2) & 3, k & 3
    return jnp.where(row == 96 * y + 12 * z + 3 * q + r, 1.0, 0.0)


def pack(slot, taps, half):
    first = half == 0
    low_lanes = lanes((14, 128)) < 64
    for r, w in enumerate(taps):
        slot[pl.ds(r, 27, stride=3), :] = jnp.where(first, w[:, :128], w[:, 128:256])
        rest = w[:, 256:]
        turned = half_roll(rest)
        low = jnp.where(first, rest, turned)[:14]
        high = jnp.concatenate([jnp.where(first, turned, rest)[14:], jnp.zeros((1, 128), F32)], axis=0)
        slot[pl.ds(81 + r, 14, stride=3), :] = jnp.where(low_lanes, low, high)
    slot[123:] = jnp.zeros((5, 128), F32)


def by_slice(x, gain):
    frame = lax.rem(lax.broadcasted_iota(jnp.int32, x.shape, 0) >> 3, 5)
    x = jnp.where(frame == 4, x, norm_silu(x, gain)).astype(BF16)
    return jnp.dot(x, spread_matrix().astype(BF16), preferred_element_type=F32)


def squeezed(x):
    free = lanes((80, 128)) >= 96
    kept = [jnp.where(free, pltpu.roll(x[240:], 96 - 32 * k, 1), x[80 * k : 80 * k + 80]) for k in range(3)]
    return jnp.concatenate(kept, axis=0)


def stretched(x):
    lane = lanes((80, 128))
    parts = [x[80 * k : 80 * k + 80] for k in range(3)]
    last = jnp.zeros((80, 128), F32)
    for k in range(3):
        last = jnp.where(lane >> 5 == k, pltpu.roll(parts[k], 32 + 32 * k, 1), last)
    return jnp.concatenate([jnp.where(lane < 96, part, 0.0) for part in parts] + [last], axis=0)


def ordered(x):
    return jnp.dot(x.astype(BF16), order_matrix().astype(BF16), preferred_element_type=F32).astype(BF16)


def pack_kernel(w2, video, cache1, cache2, mine, peer, out_edge, slot, wide, edge):
    ids = position()
    taps = [w2[r].astype(F32) for r in range(3)]
    for half, out in ((ids[0], mine), (1 - ids[0], peer)):
        pack(slot, taps, half)
        out[...] = slot[:124].astype(BF16)
    upper = ids[0] == 1
    put(wide, 0, video[...].astype(F32).reshape(256, 384))
    put(wide, 256, cache1[ids[1]].astype(F32).reshape(64, 384))
    put(wide, 320, cache2[...].astype(F32).reshape(128, 384))

    def column(f, low, high):
        return jnp.where(upper, every(wide, 64 * f + high, 8), every(wide, 64 * f + low, 8))

    for c in range(2):
        for f in range(5):
            at = 40 * c + 8 * f
            edge[at : at + 8] = column(f, c, 6 + c)
    for f in range(2):
        edge[80 + 8 * f : 88 + 8 * f] = column(5 + f, 0, 7)
    out_edge[...] = edge[...].astype(BF16)


def send_kernel(
    w1, video, cache1, cache2, gain1, bias1, gain2,
    out1, out, out_cache, out_vec,
    slot, wide, rows,
):
    ids = position()
    order = order_matrix().astype(BF16)
    taps1 = [jnp.dot(w1[r], order, preferred_element_type=F32) for r in range(3)]
    pack(slot, taps1, ids[1])
    packed = slot[:124].astype(BF16)
    for n in range(8):
        out1[n] = packed

    put(wide, 0, video[...].astype(F32).reshape(256, 384))
    put(wide, 256, cache1[ids[1]].astype(F32).reshape(64, 384))
    put(wide, 320, cache2[...].astype(F32).reshape(128, 384))
    for c in range(8):
        for f in range(5):
            at = 40 * c + 8 * f
            rows[at : at + 8] = every(wide, 64 * f + c, 8)
    slices = by_slice(rows[...], gain1[...].reshape(1, 384))
    for q in range(4):
        out[q] = squeezed(slices[:, 128 * q : 128 * q + 128]).astype(BF16)
    for c in range(8):
        for f in range(2):
            at = 16 * c + 8 * f
            rows[at : at + 8] = every(wide, 320 + 64 * f + c, 8)
    out_cache[...] = ordered(rows[0:128]).reshape(8, 16, 384)
    vectors = jnp.concatenate(
        [bias1[...].reshape(1, 384), gain2[...].reshape(1, 384), gain1[...].reshape(1, 384), jnp.zeros((5, 384), F32)],
        axis=0,
    )
    placed = jnp.dot(vectors, order_matrix(), preferred_element_type=F32, precision=lax.Precision.HIGHEST)
    out_vec[...] = jnp.concatenate([placed[:2], vectors[2:]], axis=0)


def join_kernel(axis, mine, other, out):
    at = position()[axis]
    out[at] = mine[...]
    out[1 - at] = other[...]


def turn_kernel(w0, w1, w2, w3, out, wide):
    y = position()[3]
    for d, w in enumerate((w0, w1, w2, w3)):
        at = pl.multiple_of(512 * ((y + 4 - d) & 3), 512)
        for n in range(4):
            wide[pl.ds(at + 128 * n, 124), :] = w[n].astype(F32)

    def step(row, carry):
        out[row] = wide[pl.ds(row, 16, stride=128), :].astype(BF16)
        return carry

    lax.fori_loop(0, 124, step, 0, unroll=31)


def enter_kernel(own, gain, halo, keep, give, out_cache, edge):
    ids = position()
    slices = by_slice(halo[0:80].astype(F32), gain[...].reshape(1, 384))
    for q in range(4):
        edge[q] = slices[:, 128 * q : 128 * q + 128].astype(BF16)
    for xh in range(2):
        for out, core in ((keep, ids[0]), (give, 1 - ids[0])):
            out[xh, 0:240] = own[2 * xh + core]
            out[xh, 240:320] = edge[2 * xh + core]
    out_cache[...] = ordered(halo[80:96])


def arrange_kernel(keep, got, same, across):
    ids = position()
    same[0] = keep[ids[2]]
    same[1] = got[ids[2]]
    across[0] = keep[1 - ids[2]]
    across[1] = got[1 - ids[2]]


def shifted_rows(x, p):
    if p == 1:
        return x
    axis = x.ndim - 2
    lat = lax.broadcasted_iota(jnp.int32, x.shape, axis)
    if p == 0:
        return jnp.where(lat == 0, 0.0, pltpu.roll(x, 1, axis))
    return jnp.where(lat == 7, 0.0, pltpu.roll(x, 7, axis))


def tap_of(t):
    return t // 9, (t // 3) % 3, t % 3


def field_kernel(x0, x1, x2, x3, even, odd, field):
    ids = position()
    for n, x in enumerate((x0, x1, x2, x3)):
        tm = ids[1] ^ (n & 1)
        for m in range(2):
            q = 2 * (ids[2] ^ (n >> 1)) + (ids[0] ^ m)
            packed = x[m].astype(F32)
            piece = jnp.concatenate([stretched(packed[:240]), packed[240:]], axis=0).reshape(10, 5, 8, 128)

            def place(at, begin, end):
                field[pl.ds(at, end - begin), pl.ds(2 + 4 * tm, 4)] = piece[begin:end, 0:4]
                field[pl.ds(at, end - begin), tm] = piece[begin:end, 4]

            place(2 + 8 * q, 0, 8)
            pl.when(q == 0)(lambda: place(0, 8, 10))
            pl.when(q == 3)(lambda: place(34, 8, 10))

    def spread(c, carry):
        plane = field[c]
        for p in range(3):
            moved = shifted_rows(plane, p)
            even[p, c] = moved.reshape(80, 128).astype(BF16)
            odd[p, c] = moved[1:9].reshape(64, 128).astype(BF16)
        return carry

    lax.fori_loop(0, 36, spread, 0, unroll=9)


def first_kernel(even, odd, w0, w1, w2, w3, out_own, out_peer, wide, kernel, part_a, part_b):
    ids = position()
    for d, w in enumerate((w0, w1, w2, w3)):
        at = pl.multiple_of(1024 * ((ids[3] + 4 - d) & 3), 1024)
        for z in range(8):
            wide[pl.ds(at + 128 * z, 124), :] = w[z].astype(F32)
    for t in range(27):
        for r in range(3):
            kernel[t, 32 * r : 32 * r + 32, 0:128] = wide[pl.ds(3 * t + r, 32, stride=128), :].astype(BF16)
            kernel[t, 32 * r : 32 * r + 32, 128:256] = wide[
                pl.ds(81 + 3 * (t % 14) + r, 32, stride=128), :
            ].astype(BF16)
        kernel[t, 96:128] = jnp.zeros((32, 256), BF16)

    block = 34

    def multiply(i, carry):
        at = i * block

        def window(t):
            a, p, q = tap_of(t)
            if a == 1:
                rows = odd[p, pl.ds(at + q, block)]
            else:
                rows = even[p, pl.ds(at + q, block), 8 * a : 8 * a + 64]
            return rows.reshape(block * 64, 128)

        def total(taps):
            left = jnp.concatenate([window(t) for t in taps], axis=1)
            right = kernel[taps[0] : taps[-1] + 1].reshape(128 * len(taps), 256)
            return jnp.dot(left, right, preferred_element_type=F32)

        low = total(range(0, 14))
        high = total(range(14, 27))
        part_a[pl.ds(at, block)] = (low[:, :128] + high[:, :128]).reshape(block, 64, 128)
        part_b[pl.ds(at, block)] = (low[:, 128:] + half_roll(high[:, 128:])).reshape(block, 64, 128)
        return carry

    lax.fori_loop(0, 34 // block, multiply, 0)

    low_lanes = lanes((48, 128)) < 64
    for d in range(4):
        xh, tm = d // 2, d % 2
        for out, core in ((out_own, ids[0]), (out_peer, 1 - ids[0])):
            base = 16 * xh + 9 * core

            def rows_of(part, c):
                if tm == 1:
                    return part[c, 16:64]
                return jnp.concatenate([jnp.zeros((16, 128), F32), part[c, 0:32]], axis=0)

            for j in range(9):
                out[d, j] = rows_of(part_a, base + j).astype(BF16)
            for j in range(5):
                b = rows_of(part_b, base + j)
                if j < 4:
                    b = jnp.where(low_lanes, b, half_roll(rows_of(part_b, base + j + 5)))
                out[d, 9 + j] = b.astype(BF16)


def add_kernel(x, y, *outs):
    ids = position()
    for n, out in enumerate(outs):
        d = 2 * (ids[2] ^ (n >> 1)) + (ids[1] ^ (n & 1))

        def step(j, carry):
            out[j] = (x[d, j].astype(F32) + y[d, j].astype(F32)).astype(BF16)
            return carry

        lax.fori_loop(0, 14, step, 0, unroll=2)


def middle_kernel(x0, x1, x2, x3, vec, cache, beyond, out):
    ids = position()
    low_lanes = lanes((48, 128)) < 64
    starts = ids[1] == 0

    def cached(c):
        low = beyond[...] if c == 0 else cache[c - 1]
        high = beyond[...] if c == 8 else cache[c]
        return jnp.where(ids[0] == 0, low, high)

    bias, gain = vec[0:1], vec[1:2]

    def summed(tm, j):
        mine = x0[j].astype(F32) + x2[j].astype(F32)
        other = x1[j].astype(F32) + x3[j].astype(F32)
        return jnp.where(ids[1] == tm, mine, other)

    for j in range(5):
        b0, b1 = summed(0, 9 + j), summed(1, 9 + j)
        places = [(j, jnp.where(low_lanes, b0, half_roll(b1)))]
        if j < 4:
            places.append((j + 5, jnp.where(low_lanes, half_roll(b0), b1)))
        for c, b in places:
            hidden = jnp.concatenate([summed(0, c), summed(1, c), b], axis=1) + bias
            normed = norm_silu(hidden, gain).astype(BF16)
            out[c, 16:48] = normed[16:48]
            out[c, 0:16] = jnp.where(starts, cached(c), normed[0:16])


def second_kernel(mine, other, w, bias, out_own, out_peer, even, odd, low, high):
    ids = position()
    def spread(c, carry):
        for x, core in ((mine, ids[0]), (other, 1 - ids[0])):
            plane = x[c].astype(F32).reshape(6, 8, 384)
            at = 9 * core + c
            for p in range(3):
                moved = shifted_rows(plane, p)
                even[p, at] = moved.reshape(48, 384).astype(BF16)
                odd[p, at] = moved[1:5].reshape(32, 384).astype(BF16)
        return carry

    lax.fori_loop(0, 9, spread, 0, unroll=3)

    def window(t):
        a, p, q = tap_of(t)
        if a == 1:
            rows = odd[p, q : q + 16]
        else:
            rows = even[p, q : q + 16, 8 * a : 8 * a + 32]
        return rows.reshape(512, 384)

    def kernel(t):
        a = [w[:, 3 * t + r].reshape(128, 128) for r in range(3)]
        b = [w[:, 81 + 3 * (t % 14) + r].reshape(128, 128) for r in range(3)]
        return jnp.concatenate([jnp.concatenate(a, axis=0), jnp.concatenate(b, axis=0)], axis=1)

    for begin, end, total in ((0, 14, low), (14, 27, high)):
        for t in range(begin, end, 2):
            taps = range(t, min(t + 2, end))
            left = jnp.concatenate([window(s) for s in taps], axis=1)
            right = jnp.concatenate([kernel(s) for s in taps], axis=0)
            product = jnp.dot(left, right, preferred_element_type=F32)
            if t == begin:
                total[...] = product
            else:
                total[...] += product

    first = ids[0] == 0
    bias = bias[...].reshape(1, 384)
    rest = bias[:, 256:]
    bias_a = jnp.where(first, bias[:, :128], bias[:, 128:256])
    bias_b = jnp.where(first, rest, half_roll(rest))
    low[:, :128] = low[:, :128] + high[:, :128] + bias_a
    low[:, 128:] = low[:, 128:] + half_roll(high[:, 128:]) + bias_b
    own = pl.multiple_of(256 * ids[0], 256)
    peer = pl.multiple_of(256 - 256 * ids[0], 256)
    out_own[...] = low[pl.ds(own, 256)]
    out_peer[...] = low[pl.ds(peer, 256)]


def last_kernel(own, peer, video, out, rows):
    ids = position()
    first = ids[0] == 0
    low_lanes = lanes((256, 128)) < 64
    rows[0] = jnp.where(first, own[:, :128], peer[:, :128])
    rows[1] = jnp.where(first, peer[:, :128], own[:, :128])
    b0 = jnp.where(first, own[:, 128:], peer[:, 128:])
    b1 = jnp.where(first, peer[:, 128:], own[:, 128:])
    rows[2] = jnp.where(low_lanes, b0, half_roll(b1))
    for f in range(4):
        for i in range(8):
            branch = every(rows, 8 * f + i, 32)
            out[f, i] = (video[f, i].astype(F32) + branch).astype(BF16)


def run(kernel, outs, scratch, args, flops=0, limit=48):
    specs = [pl.BlockSpec(memory_space=pltpu.VMEM)] * len(args)
    moved = sum(a.size * a.dtype.itemsize for a in args)
    return pl.pallas_call(
        kernel,
        out_shape=outs,
        in_specs=specs,
        out_specs=jax.tree.map(lambda _: pl.BlockSpec(memory_space=pltpu.VMEM), outs),
        scratch_shapes=scratch,
        compiler_params=pltpu.CompilerParams(vmem_limit_bytes=limit * MIB),
        cost_estimate=pl.CostEstimate(flops=flops, bytes_accessed=moved, transcendentals=0),
    )(*args)


def round_y(x):
    return [lax.ppermute(x, "y", [(i, (i + d) % 4) for i in range(4)]) for d in (1, 2, 3)]


def shape(*dims, dtype=BF16):
    return jax.ShapeDtypeStruct(dims, dtype)


def per_device(video, gain1, w1, bias1, gain2, w2, bias2, cache1, cache2):
    w1, w2 = w1.transpose(1, 0, 2), w2.transpose(1, 0, 2)
    mine2, peer2, edges = run(
        pack_kernel,
        [shape(124, 128), shape(124, 128), shape(96, 384)],
        [pltpu.VMEM((128, 128), F32), pltpu.VMEM((3, 448, 128), F32), pltpu.VMEM((96, 384), F32)],
        [w2, video, cache1, cache2],
        limit=60,
    )
    peer2 = lax.ppermute(peer2, "core", SWAP)
    pair2 = run(functools.partial(join_kernel, 0), shape(2, 124, 128), [], [mine2, peer2])
    pair2, w1 = lax.optimization_barrier((pair2, w1))
    sent1, slices, cache_own, vectors = run(
        send_kernel,
        [
            shape(8, 124, 128),
            shape(4, 240, 128),
            shape(8, 16, 384),
            shape(8, 384, dtype=F32),
        ],
        [
            pltpu.VMEM((128, 128), F32),
            pltpu.VMEM((3, 448, 128), F32),
            pltpu.VMEM((320, 384), F32),
        ],
        [w1, video, cache1, cache2, gain1, bias1, gain2],
        limit=60,
    )
    other2 = lax.ppermute(pair2, "xh", SWAP)
    quad2 = run(functools.partial(join_kernel, 2), shape(2, 2, 124, 128), [], [pair2, other2])
    quad2 = quad2.reshape(4, 124, 128)
    quad2, sent1 = lax.optimization_barrier((quad2, sent1))
    near2 = [quad2, *round_y(quad2)]
    halo = lax.ppermute(edges, LON, [(i, (i + 1) % 128 if i % 2 else (i - 1) % 128) for i in range(128)])
    turned2 = run(turn_kernel, shape(124, 16, 128), [pltpu.VMEM((2048, 128), F32)], near2)
    sent1, turned2, halo = lax.optimization_barrier((sent1, turned2, halo))
    near1 = lax.all_to_all(sent1, "z", 0, 0)
    kernel2 = lax.all_gather(turned2, "z", axis=0, tiled=False)
    keep, give, beyond = run(
        enter_kernel,
        [shape(2, 320, 128), shape(2, 320, 128), shape(16, 384)],
        [pltpu.VMEM((4, 80, 128), BF16)],
        [slices, gain1, halo],
    )
    got = lax.ppermute(give, "core", SWAP)
    same, across = run(arrange_kernel, [shape(2, 320, 128)] * 2, [], [keep, got])
    entered = [same] + [
        lax.ppermute(v, ("xh", "tm"), [(i, i ^ n) for i in range(4)]) for n, v in ((1, same), (2, across), (3, across))
    ]
    kernel1 = [near1, *round_y(near1)]
    even, odd = run(
        field_kernel,
        [shape(3, 36, 80, 128), shape(3, 36, 64, 128)],
        [pltpu.VMEM((36, 10, 8, 128), F32)],
        entered,
        limit=40,
    )
    part_own, part_peer = run(
        first_kernel,
        [shape(4, 14, 48, 128), shape(4, 14, 48, 128)],
        [
            pltpu.VMEM((4096, 128), F32),
            pltpu.VMEM((27, 128, 256), BF16),
            pltpu.VMEM((34, 64, 128), F32),
            pltpu.VMEM((34, 64, 128), F32),
        ],
        [even, odd, *kernel1],
        flops=2 * 2176 * 27 * 128 * 256,
        limit=40,
    )
    part_peer = lax.ppermute(part_peer, "core", SWAP)
    parts = run(add_kernel, [shape(14, 48, 128)] * 4, [], [part_own, part_peer])
    summands = [parts[0]] + [
        lax.ppermute(parts[n], ("xh", "tm"), [(i, i ^ n) for i in range(4)]) for n in (1, 2, 3)
    ]
    second = run(middle_kernel, shape(9, 48, 384), [], [*summands, vectors, cache_own, beyond])
    other = lax.ppermute(second, "core", SWAP)
    own, peer = run(
        second_kernel,
        [shape(256, 256, dtype=F32), shape(256, 256, dtype=F32)],
        [
            pltpu.VMEM((3, 18, 48, 384), BF16),
            pltpu.VMEM((3, 18, 32, 384), BF16),
            pltpu.VMEM((512, 256), F32),
            pltpu.VMEM((512, 256), F32),
        ],
        [second, other, kernel2, bias2],
        flops=2 * 512 * 27 * 384 * 256,
    )
    peer = lax.ppermute(peer, "core", SWAP)
    return run(last_kernel, shape(4, 8, 8, 384), [pltpu.VMEM((3, 256, 128), F32)], [own, peer, video])


def solution(mesh):
    ring = Mesh(mesh.devices.reshape(4, 8, 2, 2, 2), (*LON, "tm"))
    field = P("tm", None, LON, None)
    cache = P(None, None, LON, None)
    kernel = P(None, LON, None)
    return jax.shard_map(
        per_device,
        mesh=ring,
        in_specs=(field, P(), kernel, P(), P(), kernel, P(), cache, cache),
        out_specs=field,
        check_vma=False,
    )
```
